128 devices in a mesh: gx: 8 (over z, x_hi), gy: 8 (over y, core), gz: 2 (over x_lo).
Axes of the slice: x: 4 (x_hi: 2, x_lo: 2; x = x_hi * 2 + x_lo), y: 4, z: 4, core: 2. Of those that a mesh axis runs over, the one named last changes fastest.
Arguments:
- field: float32 [4, 2048, 2048], P('gz', 'gx', 'gy'), may hold values from -6 to 6
- start_x: float32 [2048, 256], P('gx'), may hold values from -6 to 6
- start_y: float32 [2048, 256], P('gy'), may hold values from -6 to 6
Outputs:
- basis_x: float32 [2048, 256], P('gx')
- basis_y: float32 [2048, 256], P('gy')
- core: float32 [4, 256, 256], P('gz', 'gx', 'gy')
The draws below stay inside these ranges and needn't reach their ends.
All inputs are finite; a program needn't handle non-finite values.
Results may differ from the reference program's by a relative error of at most 0.0003.
Values sent between devices are 32-bit elements; how exact they have to be, the bound alone decides.
A program may use at most 128 MiB of HBM per device.

```python
import jax
import jax.numpy as jnp
from jax import lax

NX = 2048
NY = 2048
RANK = 256
ITERS = 4
NZ = 4


def levels(key, dims, shards, least, largest):
    def one(position, blocks):
        draws = jax.random.uniform(jax.random.fold_in(jax.random.fold_in(key, 6), position), (blocks,), jnp.float32, least / len(shards), largest / len(shards))
        return jnp.repeat(jnp.exp(draws), dims[position] // blocks).reshape((-1,) + (1,) * (len(dims) - position - 1))

    loudness = one(*shards[0])
    for cut in shards[1:]:
        loudness = loudness * one(*cut)
    return loudness


def noise(key, shape, scale, limit, shards=(), held_as=jnp.bfloat16):
    level = levels(key, shape, shards, -0.22, 0.18) if shards else 1.0
    entries = jax.random.normal(key, shape, jnp.float32) * scale * level
    return jnp.minimum(jnp.maximum(entries, -limit), limit).astype(held_as)


def setup_inputs(seed: int = 0) -> dict:
    streams_of = jax.random.split(jax.random.key(seed), 4)
    field = noise(streams_of[0], (NZ, NX, NY), 1.0, 6.0, ((0, 2), (1, 8), (2, 8)), jnp.float32)
    start_x = noise(streams_of[1], (NX, RANK), 1.0, 6.0, ((0, 8),), jnp.float32)
    start_y = noise(streams_of[2], (NY, RANK), 1.0, 6.0, ((0, 8),), jnp.float32)
    return dict(field=field, start_x=start_x, start_y=start_y)


def orthonormalize(product_matrix):
    cross_gram = jnp.dot(product_matrix.T, product_matrix, precision=lax.Precision.HIGHEST)
    factor = jnp.linalg.cholesky(cross_gram)
    return lax.linalg.triangular_solve(factor, product_matrix, left_side=False, lower=True, transpose_a=True)

def subspace(gram_matrix, basis_now):
    for iteration in range(ITERS):
        basis_now = orthonormalize(jnp.dot(gram_matrix, basis_now, precision=lax.Precision.HIGHEST))
    return basis_now

def reference(field, start_x, start_y):
    gram_x = jnp.einsum('sxy,sby->xb', field, field, precision=lax.Precision.HIGHEST)
    basis_x = subspace(gram_x, start_x)
    projected = jnp.einsum('xa,sxy->asy', basis_x, field, precision=lax.Precision.HIGHEST)
    gram_y = jnp.einsum('asy,asb->yb', projected, projected, precision=lax.Precision.HIGHEST)
    basis_y = subspace(gram_y, start_y)
    core = jnp.einsum('yc,asy->sac', basis_y, projected, precision=lax.Precision.HIGHEST)
    return (basis_x, basis_y, core)
```

```python
import jax
import jax.numpy as jnp
from jax import lax
from jax.experimental import pallas as pl
from jax.experimental.pallas import tpu as pltpu
from jax.sharding import PartitionSpec as P

ITERS = 4

RANK = 256
PANEL = 32
LANES = 128
SUB = 8


def split3(v):
    hi = v.astype(jnp.bfloat16)
    rest = v - hi.astype(jnp.float32)
    mid = rest.astype(jnp.bfloat16)
    low = (rest - mid.astype(jnp.float32)).astype(jnp.bfloat16)
    return hi, mid, low


def eliminate_panel(work, base, panel):
    tiles, width = PANEL // SUB, 2 * RANK // LANES
    rows = work[pl.ds(base, PANEL), :]
    turned = pltpu.roll(rows[:, :RANK], RANK - base, 1)
    cols = [
        [jnp.broadcast_to(turned[SUB * q:SUB * q + SUB, c:c + 1], (SUB, LANES)) for q in range(tiles)]
        for c in range(PANEL)
    ]
    body = [[rows[SUB * q:SUB * q + SUB, LANES * t:LANES * t + LANES] for t in range(width)] for q in range(tiles)]
    place = lax.broadcasted_iota(jnp.int32, (SUB, LANES), 0)
    pivots = [jnp.ones((SUB, LANES), jnp.float32) for _ in range(tiles)]

    def across(tile, s):
        return jnp.broadcast_to(tile[s:s + 1, :], (SUB, LANES))

    for c in range(PANEL):
        first, s = c // SUB, c % SUB
        column = cols[c]
        pivot = across(column[first], s)
        inverse = 1.0 / pivot
        pivots[first] = jnp.where(place == s, pivot, pivots[first])
        below = [None] * tiles
        for q in range(first, tiles):
            below[q] = jnp.where(place > s, column[q], 0.0) if q == first else column[q]
        scaled = [None if b is None else b * inverse for b in below]
        for later in range(c + 1, PANEL):
            own = across(column[later // SUB], later % SUB)
            for q in range(later // SUB, tiles):
                if later == c + 1:
                    cols[later][q] = cols[later][q] - (below[q] * own) * inverse
                else:
                    cols[later][q] = cols[later][q] - scaled[q] * own
        for t in range(width):
            row = across(body[first][t], s)
            for q in range(first, tiles):
                body[q][t] = body[q][t] - scaled[q] * row
    scale = [lax.rsqrt(p) for p in pivots]
    done = jnp.concatenate(
        [jnp.concatenate([body[q][t] * scale[q] for t in range(width)], axis=1) for q in range(tiles)], axis=0
    )
    work[pl.ds(base, PANEL), :] = done
    return done


def cholesky_inverse(work, between=None):
    def step(panel, carry):
        base = pl.multiple_of(panel * PANEL, PANEL)
        if between is not None:
            between(panel)
        done = eliminate_panel(work, base, panel)
        lane = lax.broadcasted_iota(jnp.int32, (PANEL, RANK), 1)
        left = jnp.where(lane >= base + PANEL, done[:, :RANK], 0.0)
        lh, lm, ll = split3(left)
        rh, rm, rl = split3(done)
        lhs = jnp.concatenate([lh, lh, lm, lh, lm, ll], axis=0)
        rhs = jnp.concatenate([rh, rm, rh, rl, rm, rh], axis=0)
        work[...] -= lax.dot_general(lhs, rhs, (((0,), (0,)), ((), ())), preferred_element_type=jnp.float32)
        return carry

    lax.fori_loop(0, RANK // PANEL, step, 0)


def eye_tail():
    r = lax.broadcasted_iota(jnp.int32, (RANK, RANK), 0)
    c = lax.broadcasted_iota(jnp.int32, (RANK, RANK), 1)
    return jnp.where(r == c, 1.0, 0.0).astype(jnp.float32)


def chol_kernel(c_ref, w_ref, work):
    work[:, :RANK] = c_ref[...]
    work[:, RANK:] = eye_tail()
    cholesky_inverse(work)
    w_ref[...] = work[:, RANK:]


def inverse_factor(c):
    return pl.pallas_call(
        chol_kernel,
        out_shape=jax.ShapeDtypeStruct((RANK, RANK), jnp.float32),
        in_specs=[pl.BlockSpec(memory_space=pltpu.VMEM)],
        out_specs=pl.BlockSpec(memory_space=pltpu.VMEM),
        scratch_shapes=[pltpu.VMEM((RANK, 2 * RANK), jnp.float32)],
        compiler_params=pltpu.CompilerParams(vmem_limit_bytes=32 * 2**20),
    )(c)


def orthonormal_local(product_image, cross_gram):
    return lax.dot_general(
        product_image,
        inverse_factor(cross_gram),
        (((1,), (1,)), ((), ())),
        precision=lax.Precision.HIGHEST,
    )


def contract_outer(left_block, right_block):
    return lax.dot_general(
        left_block, right_block, (((0, 2), (0, 2)), ((), ())), precision=lax.Precision.HIGHEST
    )


def local(field, start_x, start_y):
    partial_gram = contract_outer(field, lax.all_gather(field, "gx", axis=1, tiled=True))
    gram_x = lax.psum(partial_gram, ("gy", "gz"))
    basis_x = start_x
    for iteration in range(ITERS):
        product_image = jnp.dot(
            gram_x,
            lax.all_gather(basis_x, "gx", axis=0, tiled=True),
            precision=lax.Precision.HIGHEST,
        )
        local_cross = jnp.dot(product_image.T, product_image, precision=lax.Precision.HIGHEST)
        cross_gram = lax.psum(local_cross, "gx")
        basis_x = orthonormal_local(product_image, cross_gram)
    rank_slice = basis_x
    projected = lax.psum_scatter(
        jnp.einsum("xa,sxy->asy", rank_slice, field, precision=lax.Precision.HIGHEST),
        "gx",
        scatter_dimension=0,
        tiled=True,
    )
    partial_gram_y = lax.dot_general(
        projected,
        lax.all_gather(projected, "gy", axis=2, tiled=True),
        (((0, 1), (0, 1)), ((), ())),
        precision=lax.Precision.HIGHEST,
    )
    gram_y = lax.psum(partial_gram_y, ("gx", "gz"))
    basis_y = start_y
    for iteration in range(ITERS):
        product_image = jnp.dot(
            gram_y,
            lax.all_gather(basis_y, "gy", axis=0, tiled=True),
            precision=lax.Precision.HIGHEST,
        )
        local_cross = jnp.dot(product_image.T, product_image, precision=lax.Precision.HIGHEST)
        cross_gram = lax.psum(local_cross, "gy")
        basis_y = orthonormal_local(product_image, cross_gram)
    rank_slice = basis_y
    core_turned = lax.psum_scatter(
        jnp.einsum("yc,asy->cas", rank_slice, projected, precision=lax.Precision.HIGHEST),
        "gy",
        scatter_dimension=0,
        tiled=True,
    )
    core = jnp.transpose(core_turned, (2, 1, 0))
    return (basis_x, basis_y, core)


def solution(mesh):
    return jax.shard_map(
        local,
        mesh=mesh,
        in_specs=(P("gz", "gx", "gy"), P("gx", None), P("gy", None)),
        out_specs=(P("gx", None), P("gy", None), P("gz", "gx", "gy")),
        check_vma=False,
    )
```
